32 devices in a mesh: dp: 8 (over z, x), row: 2 (over y), col: 2 (over core).
Axes of the slice: x: 2, y: 2, z: 4, core: 2. Of those that a mesh axis runs over, the one named last changes fastest.
Arguments:
- block_in: bfloat16 [3072, 768], P('dp'), may hold values from -6 to 6
- lengths: int32 [4], replicated, may hold values from 1 to 1536, as said below
- attend_in: bfloat16 [768, 2304], P('col', 'row'), may hold values from -0.21875 to 0.21875
- query_bias: float32 [768], replicated, may hold values from -1.75 to 1.75
- value_bias: float32 [768], replicated, may hold values from -1.75 to 1.75
- attend_out: bfloat16 [768, 768], P('col', 'row'), may hold values from -0.875 to 0.875
- out_bias: float32 [768], replicated, may hold values from -1.75 to 1.75
- gain_first: float32 [768], replicated, may hold values from 0.5 to 1.5
- shift_first: float32 [768], replicated, may hold values from -1.75 to 1.75
- gain_second: float32 [768], replicated, may hold values from 0.5 to 1.5
- shift_second: float32 [768], replicated, may hold values from -1.75 to 1.75
- up_weight: bfloat16 [768, 3072], P('col', 'row'), may hold values from -0.21875 to 0.21875
- up_bias: float32 [3072], replicated, may hold values from -1.75 to 1.75
- down_weight: bfloat16 [3072, 768], P('col', 'row'), may hold values from -0.109375 to 0.109375
- down_bias: float32 [768], replicated, may hold values from -1.75 to 1.75
- grad_out: bfloat16 [3072, 768], P('dp', ('row', 'col')), may hold values from -6 to 6
Outputs:
- block_out: float32 [3072, 768], P('dp', ('row', 'col'))
- grad_in: bfloat16 [3072, 768], P('dp', ('row', 'col'))
- grad_attend_in: float32 [768, 2304], P('col', 'row')
- grad_query_bias: float32 [768], replicated
- grad_value_bias: float32 [768], replicated
- grad_attend_out: float32 [768, 768], P('col', 'row')
- grad_out_bias: float32 [768], replicated
- grad_gain_first: float32 [768], replicated
- grad_shift_first: float32 [768], replicated
- grad_gain_second: float32 [768], replicated
- grad_shift_second: float32 [768], replicated
- grad_up_weight: float32 [768, 3072], P('col', 'row')
- grad_up_bias: float32 [3072], replicated
- grad_down_weight: float32 [3072, 768], P('col', 'row')
- grad_down_bias: float32 [768], replicated
The draws below stay inside these ranges and needn't reach their ends.
Inputs may be any that keep to these rules, and one draw needn't show every extreme that they name: The lengths sum to 3072; exactly one sequence, neither the first nor the last, has 1536 tokens; no sequence ends at a multiple of 384 except the last.
All inputs are finite; a program needn't handle non-finite values.
Results may differ from the reference program's by a relative error of at most 0.025.
Values may be sent and summed in bfloat16 or wider, within the bound.
A program may use at most 128 MiB of HBM per device.

```python
import jax
import jax.numpy as jnp
from jax import lax

D = 768
H = 12
HD = 64
FF = 3072
TOK_DEV = 384
TOKENS = 3072
MAXLEN = 1536
SPAN = 4
NSEQ = 4


def draw_lengths(key, part):
    key = jax.random.fold_in(key, 5)
    first_key, second_key = jax.random.split(key)
    count = NSEQ - 1
    remaining = TOKENS - MAXLEN
    typical = remaining // count
    jitter = max(typical // 4, 0)
    marks = jnp.arange(count + 1, dtype=jnp.int32)
    ends = marks * remaining // count + jax.random.randint(first_key, (count + 1,), -jitter, jitter + 1, dtype=jnp.int32)
    interior = (marks >= 1) & (marks <= count - 1)
    ends = jnp.where(marks == 0, 0, jnp.where(marks == count, remaining, ends))
    clashing = interior & ((ends % TOK_DEV == 0) | ((ends + MAXLEN) % TOK_DEV == 0))
    ends = ends - clashing.astype(jnp.int32)
    others = ends[1:] - ends[:-1]
    long_at = jax.random.randint(second_key, (), 1, count, dtype=jnp.int32)
    slots = jnp.arange(NSEQ, dtype=jnp.int32)
    before = jnp.take(others, jnp.clip(slots, 0, count - 1))
    after = jnp.take(others, jnp.clip(slots - 1, 0, count - 1))
    result = jnp.where(slots < long_at, before, jnp.where(slots == long_at, MAXLEN, after))
    return result.astype(jnp.int32)


def block_levels(stream_key, dims, cuts, low, high):
    factor_of, own = 1.0, jax.random.fold_in(stream_key, 6)
    for axis_at, parts in cuts:
        heights = jnp.exp(jax.random.uniform(jax.random.fold_in(own, axis_at), (parts,), jnp.float32, low / len(cuts), high / len(cuts)))
        factor_of = factor_of * jnp.repeat(heights, dims[axis_at] // parts).reshape([-1 if axis == axis_at else 1 for axis in range(len(dims))])
    return factor_of


def gaussian(rng, dims, scale, most, cuts=(), kind=jnp.bfloat16):
    values = scale * jax.random.normal(rng, dims, jnp.float32)
    if cuts:
        values = values * block_levels(rng, dims, cuts, -0.22, 0.18)
    return jnp.clip(values, -most, most).astype(kind)


def setup_inputs(seed: int = 0) -> dict:
    arg_keys = jax.random.split(jax.random.key(seed), 17)
    return {
        "block_in": gaussian(arg_keys[0], (TOKENS, D), 1.0, 6.0, ((0, 8),)),
        "lengths": draw_lengths(jax.random.fold_in(arg_keys[16], 71), 0),
        "attend_in": gaussian(arg_keys[2], (D, 3 * D), D ** -0.5, 0.21875, ((0, 2), (1, 2))),
        "query_bias": gaussian(arg_keys[3], (D,), 0.3, 1.75, (), jnp.float32),
        "value_bias": gaussian(arg_keys[4], (D,), 0.3, 1.75, (), jnp.float32),
        "attend_out": gaussian(arg_keys[5], (D, D), (D // 16) ** -0.5, 0.875, ((0, 2), (1, 2))),
        "out_bias": gaussian(arg_keys[6], (D,), 0.3, 1.75, (), jnp.float32),
        "gain_first": jnp.clip(1.0 + 0.1 * jax.random.normal(arg_keys[7], (D,), jnp.float32), 0.5, 1.5),
        "shift_first": gaussian(arg_keys[8], (D,), 0.3, 1.75, (), jnp.float32),
        "gain_second": jnp.clip(1.0 + 0.1 * jax.random.normal(arg_keys[9], (D,), jnp.float32), 0.5, 1.5),
        "shift_second": gaussian(arg_keys[10], (D,), 0.3, 1.75, (), jnp.float32),
        "up_weight": gaussian(arg_keys[11], (D, FF), D ** -0.5, 0.21875, ((0, 2), (1, 2))),
        "up_bias": gaussian(arg_keys[12], (FF,), 0.3, 1.75, (), jnp.float32),
        "down_weight": gaussian(arg_keys[13], (FF, D), FF ** -0.5, 0.109375, ((0, 2), (1, 2))),
        "down_bias": gaussian(arg_keys[14], (D,), 0.3, 1.75, (), jnp.float32),
        "grad_out": gaussian(arg_keys[15], (TOKENS, D), 1.0, 6.0, ((0, 8), (1, 4))),
    }


EPSILON = 1e-05
FLOOR = -1e+30

@jax.custom_vjp
def low(v):
    return lax.optimization_barrier(v.astype(jnp.bfloat16)).astype(jnp.float32)

@jax.custom_vjp
def low_back(v):
    return v

def low_keep(v):
    return (low(v), None)

def low_pass(kept, grad):
    return (grad,)

def back_keep(v):
    return (v, None)

def back_low(kept, grad):
    return (low(grad),)
low.defvjp(low_keep, low_pass)
low_back.defvjp(back_keep, back_low)

def layer_norm(stream, norm_gain, norm_shift):
    center = lax.optimization_barrier(jnp.mean(stream, axis=-1, keepdims=True))
    centred = stream - center
    spread = lax.optimization_barrier(jnp.mean(centred * centred, axis=-1, keepdims=True))
    return centred * lax.rsqrt(spread + EPSILON) * norm_gain + norm_shift

def smooth_gate(values):
    return jax.nn.gelu(values, approximate=True)

def product(left_side, right_side):
    return jnp.dot(left_side, right_side, precision=lax.Precision.HIGHEST)

def sequence_ids(positions, lengths):
    bounds = jnp.cumsum(lengths)
    return lax.optimization_barrier(jnp.sum((bounds[None, :] <= positions[:, None]).astype(jnp.int32), axis=1))

def attention(queries, keys, values, lengths):
    reach = SPAN * TOK_DEV
    blocks = TOKENS // TOK_DEV
    score_scale = HD ** (-0.5)
    padding = jnp.zeros((reach, H, HD), jnp.float32)
    keys_all = jnp.concatenate([padding, keys])
    values_all = jnp.concatenate([padding, values])
    positions = jnp.arange(TOKENS, dtype=jnp.int32)
    seq_of = sequence_ids(positions, lengths)
    key_pos = jnp.arange(-reach, TOKENS, dtype=jnp.int32)
    key_seq = jnp.concatenate([jnp.full((reach,), -1, jnp.int32), seq_of])

    def one_block(block_index):
        start = (block_index * TOK_DEV).astype(jnp.int32)
        q_block = lax.dynamic_slice_in_dim(queries, start, TOK_DEV, 0)
        k_block = lax.dynamic_slice_in_dim(keys_all, start, reach + TOK_DEV, 0)
        v_block = lax.dynamic_slice_in_dim(values_all, start, reach + TOK_DEV, 0)
        q_pos = lax.dynamic_slice_in_dim(positions, start, TOK_DEV, 0)
        q_seq = lax.dynamic_slice_in_dim(seq_of, start, TOK_DEV, 0)
        k_pos = lax.dynamic_slice_in_dim(key_pos, start, reach + TOK_DEV, 0)
        k_seq = lax.dynamic_slice_in_dim(key_seq, start, reach + TOK_DEV, 0)
        allowed = (q_seq[:, None] == k_seq[None, :]) & (k_pos[None, :] <= q_pos[:, None])
        raw = jnp.einsum('qhd,khd->hqk', q_block, k_block, precision=lax.Precision.HIGHEST)
        scores = jnp.where(allowed[None], low_back(raw) * score_scale, FLOOR)
        weights = jax.nn.softmax(scores, axis=-1)
        return jnp.einsum('hqk,khd->qhd', low(weights), v_block, precision=lax.Precision.HIGHEST)
    mixed = lax.map(jax.checkpoint(one_block), jnp.arange(blocks, dtype=jnp.int32))
    return mixed.reshape(TOKENS, H * HD)

def forward(stream, attend_in, query_bias, value_bias, attend_out, out_bias, gain_first, shift_first, gain_second, shift_second, up_weight, up_bias, down_weight, down_bias, lengths):
    h_first = low(layer_norm(stream, gain_first, shift_first))
    qkv_bias = jnp.concatenate([query_bias, jnp.zeros_like(query_bias), value_bias])
    qkv = low(low_back(product(h_first, attend_in) + qkv_bias)).reshape(TOKENS, 3, H, HD)
    mixed = low(low_back(attention(qkv[:, 0], qkv[:, 1], qkv[:, 2], lengths)))
    branch = low_back(product(mixed, attend_out) + out_bias)
    r_first = stream + branch
    h_second = low(layer_norm(r_first, gain_second, shift_second))
    gate_in = low_back(product(h_second, up_weight) + up_bias)
    hidden = low(smooth_gate(gate_in))
    return r_first + low_back(product(hidden, down_weight) + down_bias)

def reference(block_in, lengths, attend_in, query_bias, value_bias, attend_out, out_bias, gain_first, shift_first, gain_second, shift_second, up_weight, up_bias, down_weight, down_bias, grad_out):
    floats = (block_in, attend_in, query_bias, value_bias, attend_out, out_bias, gain_first, shift_first, gain_second, shift_second, up_weight, up_bias, down_weight, down_bias)
    floats = tuple((item.astype(jnp.float32) for item in floats))

    def closed(*params):
        return forward(*params, lengths)
    result, pullback = jax.vjp(closed, *floats)
    grads = pullback(grad_out.astype(jnp.float32))
    return (result, grads[0].astype(jnp.bfloat16), grads[1], grads[2], grads[3], grads[4], grads[5], grads[6], grads[7], grads[8], grads[9], grads[10], grads[11], grads[12], grads[13])
```

```python
import functools

import jax
import jax.numpy as jnp
from jax import lax
from jax.experimental import pallas as pl
from jax.experimental.pallas import tpu as pltpu
from jax.sharding import PartitionSpec as P

H = 12
LONGEST = 4096
EPSILON = 1e-05
FLOOR = -1e30
BF = jnp.bfloat16
F32 = jnp.float32
GRID = ("row", "col")
SWAP = [(0, 1), (1, 0)]
TRANSPOSE = [(0, 0), (1, 2), (2, 1), (3, 3)]
TO_FLIPPED = [(0, 1), (1, 3), (2, 0), (3, 2)]
FROM_FLIPPED = [(0, 2), (1, 0), (2, 3), (3, 1)]


def mm(a, b):
    return jnp.dot(a, b, preferred_element_type=F32)


def mm_nt(a, b):
    return lax.dot_general(a, b, (((1,), (1,)), ((), ())), preferred_element_type=F32)


def mm_tn(a, b):
    return lax.dot_general(a, b, (((0,), (0,)), ((), ())), preferred_element_type=F32)


def cut(source, index, extent, axis):
    return lax.dynamic_slice_in_dim(source, index * extent, extent, axis)


def normalise(stream):
    centred = stream - jnp.mean(stream, axis=-1, keepdims=True)
    inverse = lax.rsqrt(jnp.mean(centred * centred, axis=-1, keepdims=True) + EPSILON)
    return centred * inverse, inverse


def smooth_gate(values):
    return jax.nn.gelu(values, approximate=True)


def forward_kernel(base_ref, q_ref, kv_ref, start_ref, out_ref, log_ref, *, heads, size, rows):
    width = heads * size
    keys = kv_ref.shape[0]
    scale = size**-0.5
    first_key = base_ref[0]
    first_query = base_ref[1]

    @pl.loop(0, q_ref.shape[0] // rows)
    def _(block):
        at = pl.ds(pl.multiple_of(block * rows, rows), rows)
        k_pos = first_key + lax.broadcasted_iota(jnp.int32, (rows, keys), 1)
        q_pos = first_query + block * rows + lax.broadcasted_iota(jnp.int32, (rows, keys), 0)
        allowed = (k_pos >= start_ref[at, :]) & (k_pos <= q_pos)
        outs, logs = [], []
        for head in range(heads):
            lo = head * size
            scores = mm_nt(q_ref[at, lo : lo + size], kv_ref[:, lo : lo + size]) * scale
            scores = jnp.where(allowed, scores, FLOOR)
            top = jnp.max(scores, axis=1, keepdims=True)
            weights = jnp.exp(scores - top)
            total = jnp.sum(weights, axis=1, keepdims=True)
            mixed = mm(weights.astype(BF), kv_ref[:, width + lo : width + lo + size])
            outs.append(mixed / total)
            logs.append(top + jnp.log(total))
        out_ref[at, :] = jnp.concatenate(outs, axis=1).astype(BF)
        log_ref[at, :] = jnp.concatenate(logs, axis=1)


def query_kernel(
    base_ref, q_ref, kv_ref, start_ref, log_ref, delta_ref, do_ref, dq_ref, *, heads, size, rows
):
    width = heads * size
    keys = kv_ref.shape[0]
    scale = size**-0.5
    first_key = base_ref[0]
    first_query = base_ref[1]

    @pl.loop(0, q_ref.shape[0] // rows)
    def _(block):
        at = pl.ds(pl.multiple_of(block * rows, rows), rows)
        k_pos = first_key + lax.broadcasted_iota(jnp.int32, (rows, keys), 1)
        q_pos = first_query + block * rows + lax.broadcasted_iota(jnp.int32, (rows, keys), 0)
        allowed = (k_pos >= start_ref[at, :]) & (k_pos <= q_pos)
        outs = []
        for head in range(heads):
            lo = head * size
            keys_here = kv_ref[:, lo : lo + size]
            scores = mm_nt(q_ref[at, lo : lo + size], keys_here) * scale
            scores = jnp.where(allowed, scores, FLOOR)
            weights = jnp.exp(scores - log_ref[at, head : head + 1])
            pulled = mm_nt(do_ref[at, lo : lo + size], kv_ref[:, width + lo : width + lo + size])
            d_scores = weights * (pulled - delta_ref[at, head : head + 1]) * scale
            outs.append(mm(d_scores.astype(BF), keys_here))
        dq_ref[at, :] = jnp.concatenate(outs, axis=1).astype(BF)


def key_kernel(
    base_ref, qo_ref, do_ref, kv_ref, start_ref, log_ref, delta_ref, dkv_ref, *, heads, size, rows
):
    width = heads * size
    queries = qo_ref.shape[0]
    scale = size**-0.5
    first_query = base_ref[0]
    first_key = base_ref[1]

    @pl.loop(0, kv_ref.shape[0] // rows)
    def _(block):
        at = pl.ds(pl.multiple_of(block * rows, rows), rows)
        q_pos = first_query + lax.broadcasted_iota(jnp.int32, (rows, queries), 1)
        k_pos = first_key + block * rows + lax.broadcasted_iota(jnp.int32, (rows, queries), 0)
        allowed = (k_pos >= start_ref[0:1, :]) & (k_pos <= q_pos)
        d_keys, d_values = [], []
        for head in range(heads):
            lo = head * size
            queries_here = qo_ref[:, lo : lo + size]
            d_out = do_ref[:, lo : lo + size]
            scores = mm_nt(kv_ref[at, lo : lo + size], queries_here) * scale
            scores = jnp.where(allowed, scores, FLOOR)
            weights = jnp.exp(scores - log_ref[head : head + 1, :])
            d_values.append(mm(weights.astype(BF), d_out))
            pulled = mm_nt(kv_ref[at, width + lo : width + lo + size], d_out)
            d_scores = weights * (pulled - delta_ref[head : head + 1, :]) * scale
            d_keys.append(mm(d_scores.astype(BF), queries_here))
        dkv_ref[at, :] = jnp.concatenate(d_keys + d_values, axis=1).astype(BF)


def local_kernel(body, out_shape, operands, cost):
    in_vmem = pl.BlockSpec(memory_space=pltpu.VMEM)
    many = isinstance(out_shape, tuple)
    return pl.pallas_call(
        body,
        out_shape=out_shape,
        in_specs=[pl.BlockSpec(memory_space=pltpu.SMEM)] + [in_vmem] * (len(operands) - 1),
        out_specs=(in_vmem,) * len(out_shape) if many else in_vmem,
        compiler_params=pltpu.CompilerParams(vmem_limit_bytes=48 * 1024 * 1024),
        cost_estimate=pl.CostEstimate(
            flops=cost, bytes_accessed=8 << 20, transcendentals=cost // 256
        ),
    )(*operands)


def shards(
    block_in,
    lengths,
    attend_in,
    query_bias,
    value_bias,
    attend_out,
    out_bias,
    gain_first,
    shift_first,
    gain_second,
    shift_second,
    up_weight,
    up_bias,
    down_weight,
    down_bias,
    grad_out,
):
    row = lax.axis_index("row")
    col = lax.axis_index("col")
    place = row * 2 + col
    group = lax.axis_index("dp")
    groups = lax.axis_size("dp")
    tokens, model = block_in.shape
    size = model // H
    heads = H // 4
    share = model // 4
    half = model // 2
    longest = min(LONGEST, tokens * groups // 2)
    visits = min((longest - 2 + tokens) // tokens, groups - 1)
    window = (visits + 1) * tokens
    top = row == 0
    left = col == 0

    crossing = lax.ppermute(attend_in[:, half : 2 * half], "row", SWAP)
    low, high = attend_in[:, :half], attend_in[:, 2 * half :]
    q_half = jnp.where(top, low, crossing)
    k_half = jnp.where(top, high, low)
    v_half = jnp.where(top, crossing, high)
    in_mine = jnp.concatenate([cut(w, col, share, 1) for w in (q_half, k_half, v_half)], axis=1)
    in_other = jnp.concatenate(
        [cut(w, 1 - col, share, 1) for w in (q_half, k_half, v_half)], axis=1
    )
    in_other = lax.ppermute(in_other, "col", SWAP)
    in_own = jnp.concatenate(
        [jnp.where(left, in_mine, in_other), jnp.where(left, in_other, in_mine)], axis=0
    )

    hidden_share = up_weight.shape[1] // 2
    up_mine = cut(up_weight, col, hidden_share, 1)
    up_other = lax.ppermute(cut(up_weight, 1 - col, hidden_share, 1), "col", SWAP)
    up_own = jnp.concatenate(
        [jnp.where(left, up_mine, up_other), jnp.where(left, up_other, up_mine)], axis=0
    )

    def rows_of(at):
        return jnp.concatenate(
            [cut(attend_out, at, share, 0), cut(down_weight, at, hidden_share, 0)], axis=0
        )

    part_a = lax.ppermute(rows_of(row), GRID, TRANSPOSE)
    part_b = lax.ppermute(rows_of(1 - row), GRID, TO_FLIPPED)
    rows_own = jnp.concatenate(
        [jnp.where(left, part_a, part_b), jnp.where(left, part_b, part_a)], axis=1
    )
    out_own, down_own = rows_own[:share], rows_own[share:]
    grad_full = lax.all_gather(grad_out, GRID, axis=1, tiled=True)

    bounds = jnp.cumsum(lengths)
    everywhere = jnp.arange(tokens * groups, dtype=jnp.int32)
    starts = jnp.max(
        jnp.where(bounds[None, :] <= everywhere[:, None], bounds[None, :], 0), axis=1
    )
    start_own = cut(starts, group, tokens, 0)

    stream = block_in.astype(F32)
    n_first, inverse_first = normalise(stream)
    h_first = (n_first * gain_first + shift_first).astype(BF)
    bias_own = jnp.concatenate(
        [
            cut(query_bias, place, share, 0),
            jnp.zeros((share,), F32),
            cut(value_bias, place, share, 0),
        ]
    )
    qkv = (mm(h_first, in_own) + bias_own).astype(BF)
    queries, pair = qkv[:, :share], qkv[:, share:]
    all_pairs = lax.all_gather(pair, "dp", axis=0, tiled=True)
    first_group = jnp.maximum(group - visits, 0)
    pairs = lax.dynamic_slice_in_dim(all_pairs, first_group * tokens, window, 0)
    key_base = jnp.stack([first_group * tokens, group * tokens])
    shape = dict(heads=heads, size=size, rows=128)
    work = 4 * tokens * window * share
    mixed, log_total = local_kernel(
        functools.partial(forward_kernel, **shape),
        (
            jax.ShapeDtypeStruct((tokens, share), BF),
            jax.ShapeDtypeStruct((tokens, heads), F32),
        ),
        (key_base, queries, pairs, start_own[:, None]),
        work,
    )
    branch = lax.psum(mm(mixed, out_own).astype(BF), GRID).astype(F32) + out_bias
    r_first = stream + branch

    n_second, inverse_second = normalise(r_first)
    h_second = (n_second * gain_second + shift_second).astype(BF)
    gate_in = mm(h_second, up_own) + cut(up_bias, place, hidden_share, 0)
    hidden32, gate_pull = jax.vjp(smooth_gate, gate_in)
    hidden = hidden32.astype(BF)
    down_share = lax.psum_scatter(
        mm(hidden, down_own).astype(BF), GRID, scatter_dimension=1, tiled=True
    ).astype(F32)
    block_out = cut(r_first, place, share, 1) + (down_share + cut(down_bias, place, share, 0))

    d_gate = gate_pull(mm_nt(grad_full, down_own))[0].astype(BF)
    d_second = lax.psum(mm_nt(d_gate, up_own).astype(BF), GRID).astype(F32)

    queries_out = lax.all_gather(
        jnp.concatenate([queries, mixed], axis=1), "dp", axis=0, tiled=True
    )
    all_logs = lax.all_gather(log_total, "dp", axis=0, tiled=True)

    acts = jnp.concatenate([hidden, mixed], axis=1)
    acts_a = lax.ppermute(acts, GRID, TRANSPOSE)
    acts_b = lax.ppermute(acts, GRID, FROM_FLIPPED)
    acts_0 = jnp.where(top, acts_a, acts_b)
    acts_1 = jnp.where(top, acts_b, acts_a)
    hidden_half = jnp.concatenate([acts_0[:, :hidden_share], acts_1[:, :hidden_share]], axis=1)
    mixed_half = jnp.concatenate([acts_0[:, hidden_share:], acts_1[:, hidden_share:]], axis=1)
    d_gate_half = lax.all_gather(d_gate, "col", axis=1, tiled=True)

    g_down = mm_tn(hidden_half, cut(grad_full, row, half, 1)).astype(BF)
    g_up = mm_tn(cut(h_second, col, half, 1), d_gate_half).astype(BF)
    g_down, g_up = lax.psum((g_down, g_up), "dp")

    e_second = d_second * gain_second
    d_norm = inverse_second * (
        e_second
        - jnp.mean(e_second, axis=1, keepdims=True)
        - n_second * jnp.mean(e_second * n_second, axis=1, keepdims=True)
    )
    d_r_first = grad_full.astype(F32) + d_norm
    d_branch = d_r_first.astype(BF)
    d_mixed = mm_nt(d_branch, out_own).astype(BF)

    all_d = lax.all_gather(d_mixed, "dp", axis=0, tiled=True)
    delta = jnp.sum(
        (d_mixed.astype(F32) * mixed.astype(F32)).reshape(tokens, heads, size), axis=2
    )
    d_query = local_kernel(
        functools.partial(query_kernel, **shape),
        jax.ShapeDtypeStruct((tokens, share), BF),
        (key_base, queries, pairs, start_own[:, None], log_total, delta, d_mixed),
        6 * tokens * window * share,
    )
    last_start = jnp.minimum(group, groups - 1 - visits) * tokens
    later_qo = lax.dynamic_slice_in_dim(queries_out, last_start, window, 0)
    later_d = lax.dynamic_slice_in_dim(all_d, last_start, window, 0)
    later_log = lax.dynamic_slice_in_dim(all_logs, last_start, window, 0).T
    later_start = lax.dynamic_slice_in_dim(starts, last_start, window, 0)[None, :]
    later_delta = jnp.sum(
        (later_d.astype(F32) * later_qo[:, share:].astype(F32)).reshape(window, heads, size),
        axis=2,
    ).T
    d_pair = local_kernel(
        functools.partial(key_kernel, **shape),
        jax.ShapeDtypeStruct((tokens, 2 * share), BF),
        (
            jnp.stack([last_start, group * tokens]),
            later_qo,
            later_d,
            pair,
            later_start,
            later_log,
            later_delta,
        ),
        8 * tokens * window * share,
    )
    d_keys, d_values = d_pair[:, :share], d_pair[:, share:]
    d_qkv = jnp.concatenate([d_query, d_pair], axis=1)

    d_first = mm_nt(d_qkv, in_own)
    e_part = d_first * gain_first
    stats = jnp.concatenate(
        [
            jnp.sum(e_part, axis=1, keepdims=True),
            jnp.sum(e_part * n_first, axis=1, keepdims=True),
            jnp.zeros((tokens, 62), F32),
        ],
        axis=1,
    )
    sent = jnp.concatenate(
        [
            piece
            for at in range(4)
            for piece in (d_first[:, at * share : (at + 1) * share], stats)
        ],
        axis=1,
    ).astype(BF)
    d_share = lax.psum_scatter(sent, GRID, scatter_dimension=1, tiled=True).astype(F32)
    mean_e = d_share[:, share : share + 1] / model
    mean_en = d_share[:, share + 1 : share + 2] / model
    d_share = d_share[:, :share]
    n_share = cut(n_first, place, share, 1)
    grad_in = (
        cut(d_r_first, place, share, 1)
        + inverse_first * (d_share * cut(gain_first, place, share, 0) - mean_e - n_share * mean_en)
    ).astype(BF)

    moved = lax.ppermute(jnp.where(top, d_values, d_query), "row", SWAP)
    kept = jnp.concatenate(
        [jnp.where(top, d_query, d_keys), moved, jnp.where(top, d_keys, d_values)], axis=1
    )
    both = lax.all_gather(kept, "col", axis=0, tiled=False)
    d_cols = both.reshape(2, tokens, 3, share).transpose(1, 2, 0, 3).reshape(tokens, 3 * half)
    g_in = mm_tn(cut(h_first, col, half, 1), d_cols).astype(BF)
    g_out = mm_tn(mixed_half, cut(d_branch, row, half, 1)).astype(BF)
    g_in, g_out, g_down, g_up = lax.optimization_barrier((g_in, g_out, g_down, g_up))
    g_in, g_out = lax.psum((g_in, g_out), "dp")

    def spread(piece, extent):
        whole = jnp.zeros((extent,), F32)
        return lax.dynamic_update_slice_in_dim(whole, piece, place * piece.shape[0], 0)

    def total(array):
        return jnp.sum(array, axis=0, dtype=F32)

    ours = 0.25
    small = jnp.concatenate(
        [
            spread(total(d_query), model),
            spread(total(d_values), model),
            total(d_branch) * ours,
            spread(total(d_share * n_share), model),
            spread(total(d_share), model),
            total(d_second * n_second) * ours,
            total(d_second) * ours,
            spread(total(d_gate), up_bias.shape[0]),
            total(grad_full) * ours,
        ]
    )
    small = lax.psum(small, ("dp",) + GRID)
    parts = [small[at * model : (at + 1) * model] for at in range(7)]
    g_up_bias = small[7 * model : 7 * model + up_bias.shape[0]]
    g_down_bias = small[7 * model + up_bias.shape[0] :]
    return (
        block_out,
        grad_in,
        g_in.astype(F32),
        parts[0],
        parts[1],
        g_out.astype(F32),
        parts[2],
        parts[3],
        parts[4],
        parts[5],
        parts[6],
        g_up.astype(F32),
        g_up_bias,
        g_down.astype(F32),
        g_down_bias,
    )


def solution(mesh):
    placed = (
        P("dp", None),
        P(),
        P("col", "row"),
        P(),
        P(),
        P("col", "row"),
        P(),
        P(),
        P(),
        P(),
        P(),
        P("col", "row"),
        P(),
        P("col", "row"),
        P(),
        P("dp", ("row", "col")),
    )
    return jax.shard_map(
        shards,
        mesh=mesh,
        in_specs=placed,
        out_specs=(
            P("dp", ("row", "col")),
            P("dp", ("row", "col")),
            P("col", "row"),
            P(),
            P(),
            P("col", "row"),
            P(),
            P(),
            P(),
            P(),
            P(),
            P("col", "row"),
            P(),
            P("col", "row"),
            P(),
        ),
        check_vma=False,
    )
```

```python
import functools

import jax
import jax.numpy as jnp
from jax import lax
from jax.experimental import pallas as pl
from jax.experimental.pallas import tpu as pltpu
from jax.sharding import PartitionSpec as P

H = 12
LONGEST = 4096
EPSILON = 1e-05
FLOOR = -1e30
BF = jnp.bfloat16
F32 = jnp.float32
GRID = ("row", "col")
SWAP = [(0, 1), (1, 0)]
TRANSPOSE = [(0, 0), (1, 2), (2, 1), (3, 3)]
TO_FLIPPED = [(0, 1), (1, 3), (2, 0), (3, 2)]
FROM_FLIPPED = [(0, 2), (1, 0), (2, 3), (3, 1)]


def mm(a, b):
    return jnp.dot(a, b, preferred_element_type=F32)


def mm_nt(a, b):
    return lax.dot_general(a, b, (((1,), (1,)), ((), ())), preferred_element_type=F32)


def mm_tn(a, b):
    return lax.dot_general(a, b, (((0,), (0,)), ((), ())), preferred_element_type=F32)


def cut(source, index, extent, axis):
    return lax.dynamic_slice_in_dim(source, index * extent, extent, axis)


def normalise(stream):
    centred = stream - jnp.mean(stream, axis=-1, keepdims=True)
    inverse = lax.rsqrt(jnp.mean(centred * centred, axis=-1, keepdims=True) + EPSILON)
    return centred * inverse, inverse


def smooth_gate(values):
    return jax.nn.gelu(values, approximate=True)


def forward_kernel(base_ref, q_ref, kv_ref, start_ref, out_ref, log_ref, *, heads, size, rows):
    width = heads * size
    keys = kv_ref.shape[0]
    scale = size**-0.5
    first_key = base_ref[0]
    first_query = base_ref[1]

    @pl.loop(0, q_ref.shape[0] // rows)
    def _(block):
        at = pl.ds(pl.multiple_of(block * rows, rows), rows)
        k_pos = first_key + lax.broadcasted_iota(jnp.int32, (rows, keys), 1)
        q_pos = first_query + block * rows + lax.broadcasted_iota(jnp.int32, (rows, keys), 0)
        allowed = (k_pos >= start_ref[at, :]) & (k_pos <= q_pos)
        outs, logs = [], []
        for head in range(heads):
            lo = head * size
            scores = mm_nt(q_ref[at, lo : lo + size], kv_ref[:, lo : lo + size]) * scale
            scores = jnp.where(allowed, scores, FLOOR)
            top = jnp.max(scores, axis=1, keepdims=True)
            weights = jnp.exp(scores - top)
            total = jnp.sum(weights, axis=1, keepdims=True)
            mixed = mm(weights.astype(BF), kv_ref[:, width + lo : width + lo + size])
            outs.append(mixed / total)
            logs.append(top + jnp.log(total))
        out_ref[at, :] = jnp.concatenate(outs, axis=1).astype(BF)
        log_ref[at, :] = jnp.concatenate(logs, axis=1)


def query_kernel(
    base_ref, q_ref, kv_ref, start_ref, log_ref, delta_ref, do_ref, dq_ref, *, heads, size, rows
):
    width = heads * size
    keys = kv_ref.shape[0]
    scale = size**-0.5
    first_key = base_ref[0]
    first_query = base_ref[1]

    @pl.loop(0, q_ref.shape[0] // rows)
    def _(block):
        at = pl.ds(pl.multiple_of(block * rows, rows), rows)
        k_pos = first_key + lax.broadcasted_iota(jnp.int32, (rows, keys), 1)
        q_pos = first_query + block * rows + lax.broadcasted_iota(jnp.int32, (rows, keys), 0)
        allowed = (k_pos >= start_ref[at, :]) & (k_pos <= q_pos)
        outs = []
        for head in range(heads):
            lo = head * size
            keys_here = kv_ref[:, lo : lo + size]
            scores = mm_nt(q_ref[at, lo : lo + size], keys_here) * scale
            scores = jnp.where(allowed, scores, FLOOR)
            weights = jnp.exp(scores - log_ref[at, head : head + 1])
            pulled = mm_nt(do_ref[at, lo : lo + size], kv_ref[:, width + lo : width + lo + size])
            d_scores = weights * (pulled - delta_ref[at, head : head + 1]) * scale
            outs.append(mm(d_scores.astype(BF), keys_here))
        dq_ref[at, :] = jnp.concatenate(outs, axis=1).astype(BF)


def key_kernel(
    base_ref, qo_ref, do_ref, kv_ref, start_ref, log_ref, delta_ref, dkv_ref, *, heads, size, rows
):
    width = heads * size
    queries = qo_ref.shape[0]
    scale = size**-0.5
    first_query = base_ref[0]
    first_key = base_ref[1]

    @pl.loop(0, kv_ref.shape[0] // rows)
    def _(block):
        at = pl.ds(pl.multiple_of(block * rows, rows), rows)
        q_pos = first_query + lax.broadcasted_iota(jnp.int32, (rows, queries), 1)
        k_pos = first_key + block * rows + lax.broadcasted_iota(jnp.int32, (rows, queries), 0)
        allowed = (k_pos >= start_ref[0:1, :]) & (k_pos <= q_pos)
        d_keys, d_values = [], []
        for head in range(heads):
            lo = head * size
            queries_here = qo_ref[:, lo : lo + size]
            d_out = do_ref[:, lo : lo + size]
            scores = mm_nt(kv_ref[at, lo : lo + size], queries_here) * scale
            scores = jnp.where(allowed, scores, FLOOR)
            weights = jnp.exp(scores - log_ref[head : head + 1, :])
            d_values.append(mm(weights.astype(BF), d_out))
            pulled = mm_nt(kv_ref[at, width + lo : width + lo + size], d_out)
            d_scores = weights * (pulled - delta_ref[head : head + 1, :]) * scale
            d_keys.append(mm(d_scores.astype(BF), queries_here))
        dkv_ref[at, :] = jnp.concatenate(d_keys + d_values, axis=1).astype(BF)


def local_kernel(body, out_shape, operands, cost):
    in_vmem = pl.BlockSpec(memory_space=pltpu.VMEM)
    many = isinstance(out_shape, tuple)
    return pl.pallas_call(
        body,
        out_shape=out_shape,
        in_specs=[pl.BlockSpec(memory_space=pltpu.SMEM)] + [in_vmem] * (len(operands) - 1),
        out_specs=(in_vmem,) * len(out_shape) if many else in_vmem,
        compiler_params=pltpu.CompilerParams(vmem_limit_bytes=48 * 1024 * 1024),
        cost_estimate=pl.CostEstimate(
            flops=cost, bytes_accessed=8 << 20, transcendentals=cost // 256
        ),
    )(*operands)


def exchange(source, slots, result, sems, peers, me, count, axis):
    chunk = source.shape[0] // count
    send_one, recv_one, send_two, recv_two = sems

    def rows_at(index):
        return pl.ds(pl.multiple_of(index * chunk, chunk), chunk)

    first, second = [], []
    for k in range(1, count):
        first.append(
            pltpu.make_async_remote_copy(
                src_ref=source.at[rows_at(lax.rem(me + k, count))],
                dst_ref=slots.at[k - 1],
                send_sem=send_one.at[k - 1],
                recv_sem=recv_one.at[k - 1],
                device_id=peers(k),
                device_id_type=pl.DeviceIdType.MESH,
            )
        )
        second.append(
            pltpu.make_async_remote_copy(
                src_ref=result.at[rows_at(me)],
                dst_ref=result.at[rows_at(me)],
                send_sem=send_two.at[k - 1],
                recv_sem=recv_two.at[k - 1],
                device_id=peers(k),
                device_id_type=pl.DeviceIdType.MESH,
            )
        )
    return first, second, rows_at(me)


def greet(devices):
    barrier = pltpu.get_barrier_semaphore()
    for device in devices:
        pl.semaphore_signal(
            barrier, inc=1, device_id=device, device_id_type=pl.DeviceIdType.MESH
        )
    pl.semaphore_wait(barrier, len(devices))


def grid_device(k):
    place = lax.rem(lax.axis_index("row") * 2 + lax.axis_index("col") + k, 4)
    return {"row": place // 2, "col": lax.rem(place, 2)}


def grid_sum_kernel(source, result, slots, *sems):
    place = lax.axis_index("row") * 2 + lax.axis_index("col")
    greet([grid_device(k) for k in range(1, 4)])
    first, second, mine = exchange(source, slots, result, sems, grid_device, place, 4, GRID)
    for copy in first:
        copy.start()
    for copy in first:
        copy.wait()
    summed = source[mine, :].astype(F32)
    for k in range(3):
        summed = summed + slots[k].astype(F32)
    result[mine, :] = summed.astype(BF)
    for copy in second:
        copy.start()
    for copy in second:
        copy.wait()


def grid_sum(partial_value, collective_id):
    rows, columns = partial_value.shape
    in_vmem = pl.BlockSpec(memory_space=pltpu.VMEM)
    return pl.pallas_call(
        grid_sum_kernel,
        out_shape=jax.ShapeDtypeStruct((rows, columns), BF),
        in_specs=[in_vmem],
        out_specs=in_vmem,
        scratch_shapes=[pltpu.VMEM((3, rows // 4, columns), BF)]
        + [pltpu.SemaphoreType.DMA((3,))] * 4,
        compiler_params=pltpu.CompilerParams(
            collective_id=collective_id,
            has_side_effects=True,
            vmem_limit_bytes=24 * 1024 * 1024,
        ),
        cost_estimate=pl.CostEstimate(
            flops=4 * rows * columns, bytes_accessed=24 << 20, transcendentals=0
        ),
    )(partial_value)


def group_sum_kernel(count, source, small, result, small_out, slots, small_slots, total, *sems):
    group = lax.axis_index("dp")
    place = lax.axis_index("row") * 2 + lax.axis_index("col")

    def peers(k):
        return {"dp": lax.rem(group + k, count)}

    greet([peers(k) for k in range(1, count)] + [grid_device(k) for k in range(1, 4)])
    first, second, mine = exchange(source, slots, result, sems[:4], peers, group, count, "dp")
    send_small, recv_small, send_grid, recv_grid = sems[4:]
    small_first = [
        pltpu.make_async_remote_copy(
            src_ref=small,
            dst_ref=small_slots.at[k - 1],
            send_sem=send_small.at[k - 1],
            recv_sem=recv_small.at[k - 1],
            device_id=peers(k),
            device_id_type=pl.DeviceIdType.MESH,
        )
        for k in range(1, count)
    ]
    small_second = [
        pltpu.make_async_remote_copy(
            src_ref=total,
            dst_ref=small_out.at[place],
            send_sem=send_grid.at[k - 1],
            recv_sem=recv_grid.at[k - 1],
            device_id=grid_device(k),
            device_id_type=pl.DeviceIdType.MESH,
        )
        for k in range(1, 4)
    ]
    for copy in small_first + first:
        copy.start()
    for copy in small_first:
        copy.wait()
    gathered = jnp.zeros(small.shape, F32)
    for at in range(count):
        back = lax.rem(group - at + count, count)
        other = small_slots[jnp.maximum(back - 1, 0)]
        gathered = gathered + jnp.where(back == 0, small[...], other)
    total[...] = gathered
    small_out[place] = gathered
    for copy in small_second:
        copy.start()
    for copy in first:
        copy.wait()
    summed = source[mine, :].astype(F32)
    for k in range(count - 1):
        summed = summed + slots[k].astype(F32)
    result[mine, :] = summed.astype(BF)
    for copy in second:
        copy.start()
    for copy in small_second + second:
        copy.wait()


def group_sum(grads, small, groups):
    rows, columns = grads.shape
    if groups > 8 or rows % (16 * groups):
        return lax.psum(grads, "dp"), lax.all_gather(lax.psum(small, "dp"), GRID)
    in_vmem = pl.BlockSpec(memory_space=pltpu.VMEM)
    return pl.pallas_call(
        functools.partial(group_sum_kernel, groups),
        out_shape=(
            jax.ShapeDtypeStruct(grads.shape, BF),
            jax.ShapeDtypeStruct((4,) + small.shape, F32),
        ),
        in_specs=[in_vmem] * 2,
        out_specs=(in_vmem, in_vmem),
        scratch_shapes=[
            pltpu.VMEM((groups - 1, rows // groups, columns), BF),
            pltpu.VMEM((groups - 1,) + small.shape, F32),
            pltpu.VMEM(small.shape, F32),
        ]
        + [pltpu.SemaphoreType.DMA((groups - 1,))] * 6
        + [pltpu.SemaphoreType.DMA((3,))] * 2,
        compiler_params=pltpu.CompilerParams(
            collective_id=3, has_side_effects=True, vmem_limit_bytes=24 * 1024 * 1024
        ),
        cost_estimate=pl.CostEstimate(
            flops=8 * rows * columns, bytes_accessed=100 << 20, transcendentals=0
        ),
    )(grads, small)


def from_behind(array, by, groups):
    return lax.ppermute(
        array, "dp", [(i, i + by) for i in range(groups) if 0 <= i + by < groups]
    )


def shards(
    block_in,
    lengths,
    attend_in,
    query_bias,
    value_bias,
    attend_out,
    out_bias,
    gain_first,
    shift_first,
    gain_second,
    shift_second,
    up_weight,
    up_bias,
    down_weight,
    down_bias,
    grad_out,
):
    row = lax.axis_index("row")
    col = lax.axis_index("col")
    place = row * 2 + col
    group = lax.axis_index("dp")
    groups = lax.axis_size("dp")
    tokens, model = block_in.shape
    size = model // H
    heads = H // 4
    share = model // 4
    half = model // 2
    longest = min(LONGEST, tokens * groups // 2)
    visits = min((longest - 2 + tokens) // tokens, groups - 1)
    window = (visits + 1) * tokens
    top = row == 0
    left = col == 0

    crossing = lax.ppermute(attend_in[:, half : 2 * half], "row", SWAP)
    low, high = attend_in[:, :half], attend_in[:, 2 * half :]
    q_half = jnp.where(top, low, crossing)
    k_half = jnp.where(top, high, low)
    v_half = jnp.where(top, crossing, high)
    in_mine = jnp.concatenate([cut(w, col, share, 1) for w in (q_half, k_half, v_half)], axis=1)
    in_other = jnp.concatenate(
        [cut(w, 1 - col, share, 1) for w in (q_half, k_half, v_half)], axis=1
    )
    in_other = lax.ppermute(in_other, "col", SWAP)
    in_own = jnp.concatenate(
        [jnp.where(left, in_mine, in_other), jnp.where(left, in_other, in_mine)], axis=0
    )

    hidden_share = up_weight.shape[1] // 2
    up_mine = cut(up_weight, col, hidden_share, 1)
    up_other = lax.ppermute(cut(up_weight, 1 - col, hidden_share, 1), "col", SWAP)
    up_own = jnp.concatenate(
        [jnp.where(left, up_mine, up_other), jnp.where(left, up_other, up_mine)], axis=0
    )

    def rows_of(at):
        return jnp.concatenate(
            [cut(attend_out, at, share, 0), cut(down_weight, at, hidden_share, 0)], axis=0
        )

    part_a = lax.ppermute(rows_of(row), GRID, TRANSPOSE)
    part_b = lax.ppermute(rows_of(1 - row), GRID, TO_FLIPPED)
    rows_own = jnp.concatenate(
        [jnp.where(left, part_a, part_b), jnp.where(left, part_b, part_a)], axis=1
    )
    out_own, down_own = rows_own[:share], rows_own[share:]
    grad_full = lax.all_gather(grad_out, GRID, axis=1, tiled=True)

    bounds = jnp.cumsum(lengths)
    everywhere = jnp.arange(tokens * groups, dtype=jnp.int32)
    starts = jnp.max(
        jnp.where(bounds[None, :] <= everywhere[:, None], bounds[None, :], 0), axis=1
    )
    start_own = cut(starts, group, tokens, 0)

    stream = block_in.astype(F32)
    n_first, inverse_first = normalise(stream)
    h_first = (n_first * gain_first + shift_first).astype(BF)
    bias_own = jnp.concatenate(
        [
            cut(query_bias, place, share, 0),
            jnp.zeros((share,), F32),
            cut(value_bias, place, share, 0),
        ]
    )
    qkv = (mm(h_first, in_own) + bias_own).astype(BF)
    queries, pair = qkv[:, :share], qkv[:, share:]
    pairs = jnp.concatenate(
        [from_behind(pair, by, groups) for by in range(visits, 0, -1)] + [pair], axis=0
    )
    key_base = jnp.stack([(group - visits) * tokens, group * tokens])
    shape = dict(heads=heads, size=size, rows=128)
    work = 4 * tokens * window * share
    mixed, log_total = local_kernel(
        functools.partial(forward_kernel, **shape),
        (
            jax.ShapeDtypeStruct((tokens, share), BF),
            jax.ShapeDtypeStruct((tokens, heads), F32),
        ),
        (key_base, queries, pairs, start_own[:, None]),
        work,
    )
    branch = grid_sum(mm(mixed, out_own).astype(BF), 1).astype(F32) + out_bias
    r_first = stream + branch

    n_second, inverse_second = normalise(r_first)
    h_second = (n_second * gain_second + shift_second).astype(BF)
    gate_in = mm(h_second, up_own) + cut(up_bias, place, hidden_share, 0)
    hidden32, gate_pull = jax.vjp(smooth_gate, gate_in)
    hidden = hidden32.astype(BF)
    down_share = lax.psum_scatter(
        mm(hidden, down_own).astype(BF), GRID, scatter_dimension=1, tiled=True
    ).astype(F32)
    block_out = cut(r_first, place, share, 1) + (down_share + cut(down_bias, place, share, 0))

    d_gate = gate_pull(mm_nt(grad_full, down_own))[0].astype(BF)
    d_second = grid_sum(mm_nt(d_gate, up_own).astype(BF), 2).astype(F32)

    own_qo = jnp.concatenate([queries, mixed], axis=1)
    later_qo = jnp.concatenate(
        [own_qo] + [from_behind(own_qo, -by, groups) for by in range(1, visits + 1)], axis=0
    )
    own_log = log_total.T
    later_log = jnp.concatenate(
        [own_log] + [from_behind(own_log, -by, groups) for by in range(1, visits + 1)], axis=1
    )
    beyond = jnp.full((tokens * visits,), tokens * groups, jnp.int32)
    later_start = lax.dynamic_slice_in_dim(
        jnp.concatenate([starts, beyond]), group * tokens, window, 0
    )[None, :]

    acts = jnp.concatenate([hidden, mixed], axis=1)
    acts_a = lax.ppermute(acts, GRID, TRANSPOSE)
    acts_b = lax.ppermute(acts, GRID, FROM_FLIPPED)
    acts_0 = jnp.where(top, acts_a, acts_b)
    acts_1 = jnp.where(top, acts_b, acts_a)
    hidden_half = jnp.concatenate([acts_0[:, :hidden_share], acts_1[:, :hidden_share]], axis=1)
    mixed_half = jnp.concatenate([acts_0[:, hidden_share:], acts_1[:, hidden_share:]], axis=1)
    d_gate_half = lax.all_gather(d_gate, "col", axis=1, tiled=True)

    g_down = mm_tn(hidden_half, cut(grad_full, row, half, 1)).astype(BF)
    g_up = mm_tn(cut(h_second, col, half, 1), d_gate_half).astype(BF)
    g_down, g_up = lax.psum((g_down, g_up), "dp")

    e_second = d_second * gain_second
    d_norm = inverse_second * (
        e_second
        - jnp.mean(e_second, axis=1, keepdims=True)
        - n_second * jnp.mean(e_second * n_second, axis=1, keepdims=True)
    )
    d_r_first = grad_full.astype(F32) + d_norm
    d_branch = d_r_first.astype(BF)
    d_mixed = mm_nt(d_branch, out_own).astype(BF)

    later_d = jnp.concatenate(
        [d_mixed] + [from_behind(d_mixed, -by, groups) for by in range(1, visits + 1)], axis=0
    )
    delta = jnp.sum(
        (d_mixed.astype(F32) * mixed.astype(F32)).reshape(tokens, heads, size), axis=2
    )
    d_query = local_kernel(
        functools.partial(query_kernel, **shape),
        jax.ShapeDtypeStruct((tokens, share), BF),
        (key_base, queries, pairs, start_own[:, None], log_total, delta, d_mixed),
        6 * tokens * window * share,
    )
    later_delta = jnp.sum(
        (later_d.astype(F32) * later_qo[:, share:].astype(F32)).reshape(window, heads, size),
        axis=2,
    ).T
    d_pair = local_kernel(
        functools.partial(key_kernel, **shape),
        jax.ShapeDtypeStruct((tokens, 2 * share), BF),
        (
            jnp.stack([group * tokens, group * tokens]),
            later_qo,
            later_d,
            pair,
            later_start,
            later_log,
            later_delta,
        ),
        8 * tokens * window * share,
    )
    d_keys, d_values = d_pair[:, :share], d_pair[:, share:]
    d_qkv = jnp.concatenate([d_query, d_pair], axis=1)

    d_first = mm_nt(d_qkv, in_own)
    e_part = d_first * gain_first
    stats = jnp.concatenate(
        [
            jnp.sum(e_part, axis=1, keepdims=True),
            jnp.sum(e_part * n_first, axis=1, keepdims=True),
            jnp.zeros((tokens, 62), F32),
        ],
        axis=1,
    )
    sent = jnp.concatenate(
        [
            piece
            for at in range(4)
            for piece in (d_first[:, at * share : (at + 1) * share], stats)
        ],
        axis=1,
    ).astype(BF)
    d_share = lax.psum_scatter(sent, GRID, scatter_dimension=1, tiled=True).astype(F32)
    mean_e = d_share[:, share : share + 1] / model
    mean_en = d_share[:, share + 1 : share + 2] / model
    d_share = d_share[:, :share]
    n_share = cut(n_first, place, share, 1)
    grad_in = (
        cut(d_r_first, place, share, 1)
        + inverse_first * (d_share * cut(gain_first, place, share, 0) - mean_e - n_share * mean_en)
    ).astype(BF)

    moved = lax.ppermute(jnp.where(top, d_values, d_query), "row", SWAP)
    kept = jnp.concatenate(
        [jnp.where(top, d_query, d_keys), moved, jnp.where(top, d_keys, d_values)], axis=1
    )
    both = lax.all_gather(kept, "col", axis=0, tiled=False)
    d_cols = both.reshape(2, tokens, 3, share).transpose(1, 2, 0, 3).reshape(tokens, 3 * half)
    g_in = mm_tn(cut(h_first, col, half, 1), d_cols).astype(BF)
    g_out = mm_tn(mixed_half, cut(d_branch, row, half, 1)).astype(BF)

    def total(array):
        return jnp.sum(array, axis=0, dtype=F32)

    def own(vector):
        return cut(vector, place, vector.shape[0] // 4, 0)

    quarters = [
        total(d_query),
        total(d_values),
        own(total(d_branch)),
        own(total(d_second * n_second)),
        own(total(d_second)),
        own(total(grad_full)),
        total(d_gate),
    ]
    sums = [total(d_first * n_first), total(d_first)]
    lanes = 128
    quarter_size = 6 * share + hidden_share
    padding = jnp.zeros((40 * lanes - quarter_size - 2 * model,), F32)
    small = jnp.concatenate(quarters + sums + [padding]).reshape(40, lanes)
    grads, small = group_sum(jnp.concatenate([g_in, g_out], axis=1), small, groups)
    g_in, g_out = grads[:, : 3 * half], grads[:, 3 * half :]
    small = small.reshape(4, 40 * lanes)
    wholes = [small[:, at * share : (at + 1) * share].reshape(model) for at in range(6)]
    g_up_bias = small[:, 6 * share : quarter_size].reshape(4 * hidden_share)
    g_down_bias = wholes[5]
    firsts = jnp.sum(small[:, quarter_size : quarter_size + 2 * model], axis=0)
    parts = wholes[:3] + [firsts[:model], firsts[model:]] + wholes[3:5]
    return (
        block_out,
        grad_in,
        g_in.astype(F32),
        parts[0],
        parts[1],
        g_out.astype(F32),
        parts[2],
        parts[3],
        parts[4],
        parts[5],
        parts[6],
        g_up.astype(F32),
        g_up_bias,
        g_down.astype(F32),
        g_down_bias,
    )


def solution(mesh):
    placed = (
        P("dp", None),
        P(),
        P("col", "row"),
        P(),
        P(),
        P("col", "row"),
        P(),
        P(),
        P(),
        P(),
        P(),
        P("col", "row"),
        P(),
        P("col", "row"),
        P(),
        P("dp", ("row", "col")),
    )
    return jax.shard_map(
        shards,
        mesh=mesh,
        in_specs=placed,
        out_specs=(
            P("dp", ("row", "col")),
            P("dp", ("row", "col")),
            P("col", "row"),
            P(),
            P(),
            P("col", "row"),
            P(),
            P(),
            P(),
            P(),
            P(),
            P("col", "row"),
            P(),
            P("col", "row"),
            P(),
        ),
        check_vma=False,
    )
```

```python
import functools

import jax
import jax.numpy as jnp
from jax import lax
from jax.experimental import pallas as pl
from jax.experimental.pallas import tpu as pltpu
from jax.sharding import PartitionSpec as P

H = 12
LONGEST = 4096
EPSILON = 1e-05
FLOOR = -1e30
BF = jnp.bfloat16
F32 = jnp.float32
GRID = ("row", "col")
SWAP = [(0, 1), (1, 0)]
TRANSPOSE = [(0, 0), (1, 2), (2, 1), (3, 3)]
TO_FLIPPED = [(0, 1), (1, 3), (2, 0), (3, 2)]
FROM_FLIPPED = [(0, 2), (1, 0), (2, 3), (3, 1)]


def mm(a, b):
    return jnp.dot(a, b, preferred_element_type=F32)


def mm_nt(a, b):
    return lax.dot_general(a, b, (((1,), (1,)), ((), ())), preferred_element_type=F32)


def mm_tn(a, b):
    return lax.dot_general(a, b, (((0,), (0,)), ((), ())), preferred_element_type=F32)


def cut(source, index, extent, axis):
    return lax.dynamic_slice_in_dim(source, index * extent, extent, axis)


def normalise(stream):
    centred = stream - jnp.mean(stream, axis=-1, keepdims=True)
    inverse = lax.rsqrt(jnp.mean(centred * centred, axis=-1, keepdims=True) + EPSILON)
    return centred * inverse, inverse


def smooth_gate(values):
    return jax.nn.gelu(values, approximate=True)


def forward_kernel(base_ref, q_ref, kv_ref, start_ref, out_ref, log_ref, *, heads, size, rows):
    width = heads * size
    keys = kv_ref.shape[0]
    scale = size**-0.5
    first_key = base_ref[0]
    first_query = base_ref[1]

    @pl.loop(0, q_ref.shape[0] // rows)
    def _(block):
        at = pl.ds(pl.multiple_of(block * rows, rows), rows)
        k_pos = first_key + lax.broadcasted_iota(jnp.int32, (rows, keys), 1)
        q_pos = first_query + block * rows + lax.broadcasted_iota(jnp.int32, (rows, keys), 0)
        allowed = (k_pos >= start_ref[at, :]) & (k_pos <= q_pos)
        outs, logs = [], []
        for head in range(heads):
            lo = head * size
            scores = mm_nt(q_ref[at, lo : lo + size], kv_ref[:, lo : lo + size]) * scale
            scores = jnp.where(allowed, scores, FLOOR)
            top = jnp.max(scores, axis=1, keepdims=True)
            weights = jnp.exp(scores - top)
            total = jnp.sum(weights, axis=1, keepdims=True)
            mixed = mm(weights.astype(BF), kv_ref[:, width + lo : width + lo + size])
            outs.append(mixed / total)
            logs.append(top + jnp.log(total))
        out_ref[at, :] = jnp.concatenate(outs, axis=1).astype(BF)
        log_ref[at, :] = jnp.concatenate(logs, axis=1)


def query_kernel(
    base_ref, q_ref, kv_ref, start_ref, log_ref, delta_ref, do_ref, dq_ref, *, heads, size, rows
):
    width = heads * size
    keys = kv_ref.shape[0]
    scale = size**-0.5
    first_key = base_ref[0]
    first_query = base_ref[1]

    @pl.loop(0, q_ref.shape[0] // rows)
    def _(block):
        at = pl.ds(pl.multiple_of(block * rows, rows), rows)
        k_pos = first_key + lax.broadcasted_iota(jnp.int32, (rows, keys), 1)
        q_pos = first_query + block * rows + lax.broadcasted_iota(jnp.int32, (rows, keys), 0)
        allowed = (k_pos >= start_ref[at, :]) & (k_pos <= q_pos)
        outs = []
        for head in range(heads):
            lo = head * size
            keys_here = kv_ref[:, lo : lo + size]
            scores = mm_nt(q_ref[at, lo : lo + size], keys_here) * scale
            scores = jnp.where(allowed, scores, FLOOR)
            weights = jnp.exp(scores - log_ref[at, head : head + 1])
            pulled = mm_nt(do_ref[at, lo : lo + size], kv_ref[:, width + lo : width + lo + size])
            d_scores = weights * (pulled - delta_ref[at, head : head + 1]) * scale
            outs.append(mm(d_scores.astype(BF), keys_here))
        dq_ref[at, :] = jnp.concatenate(outs, axis=1).astype(BF)


def key_kernel(
    base_ref, qo_ref, do_ref, kv_ref, start_ref, log_ref, delta_ref, dkv_ref, *, heads, size, rows
):
    width = heads * size
    queries = qo_ref.shape[0]
    scale = size**-0.5
    first_query = base_ref[0]
    first_key = base_ref[1]

    @pl.loop(0, kv_ref.shape[0] // rows)
    def _(block):
        at = pl.ds(pl.multiple_of(block * rows, rows), rows)
        q_pos = first_query + lax.broadcasted_iota(jnp.int32, (rows, queries), 1)
        k_pos = first_key + block * rows + lax.broadcasted_iota(jnp.int32, (rows, queries), 0)
        allowed = (k_pos >= start_ref[0:1, :]) & (k_pos <= q_pos)
        d_keys, d_values = [], []
        for head in range(heads):
            lo = head * size
            queries_here = qo_ref[:, lo : lo + size]
            d_out = do_ref[:, lo : lo + size]
            scores = mm_nt(kv_ref[at, lo : lo + size], queries_here) * scale
            scores = jnp.where(allowed, scores, FLOOR)
            weights = jnp.exp(scores - log_ref[head : head + 1, :])
            d_values.append(mm(weights.astype(BF), d_out))
            pulled = mm_nt(kv_ref[at, width + lo : width + lo + size], d_out)
            d_scores = weights * (pulled - delta_ref[head : head + 1, :]) * scale
            d_keys.append(mm(d_scores.astype(BF), queries_here))
        dkv_ref[at, :] = jnp.concatenate(d_keys + d_values, axis=1).astype(BF)


def local_kernel(body, out_shape, operands, cost):
    in_vmem = pl.BlockSpec(memory_space=pltpu.VMEM)
    many = isinstance(out_shape, tuple)
    return pl.pallas_call(
        body,
        out_shape=out_shape,
        in_specs=[pl.BlockSpec(memory_space=pltpu.SMEM)] + [in_vmem] * (len(operands) - 1),
        out_specs=(in_vmem,) * len(out_shape) if many else in_vmem,
        compiler_params=pltpu.CompilerParams(vmem_limit_bytes=48 * 1024 * 1024),
        cost_estimate=pl.CostEstimate(
            flops=cost, bytes_accessed=8 << 20, transcendentals=cost // 256
        ),
    )(*operands)


def exchange(source, slots, result, sems, peers, me, count, axis):
    chunk = source.shape[0] // count
    send_one, recv_one, send_two, recv_two = sems

    def rows_at(index):
        return pl.ds(pl.multiple_of(index * chunk, chunk), chunk)

    first, second = [], []
    for k in range(1, count):
        first.append(
            pltpu.make_async_remote_copy(
                src_ref=source.at[rows_at(lax.rem(me + k, count))],
                dst_ref=slots.at[k - 1],
                send_sem=send_one.at[k - 1],
                recv_sem=recv_one.at[k - 1],
                device_id=peers(k),
                device_id_type=pl.DeviceIdType.MESH,
            )
        )
        second.append(
            pltpu.make_async_remote_copy(
                src_ref=result.at[rows_at(me)],
                dst_ref=result.at[rows_at(me)],
                send_sem=send_two.at[k - 1],
                recv_sem=recv_two.at[k - 1],
                device_id=peers(k),
                device_id_type=pl.DeviceIdType.MESH,
            )
        )
    return first, second, rows_at(me)


def greet(devices):
    barrier = pltpu.get_barrier_semaphore()
    for device in devices:
        pl.semaphore_signal(
            barrier, inc=1, device_id=device, device_id_type=pl.DeviceIdType.MESH
        )
    pl.semaphore_wait(barrier, len(devices))


def grid_device(k):
    place = lax.rem(lax.axis_index("row") * 2 + lax.axis_index("col") + k, 4)
    return {"row": place // 2, "col": lax.rem(place, 2)}


def grid_sum_kernel(source, result, slots, *sems):
    place = lax.axis_index("row") * 2 + lax.axis_index("col")
    greet([grid_device(k) for k in range(1, 4)])
    first, second, mine = exchange(source, slots, result, sems, grid_device, place, 4, GRID)
    for copy in first:
        copy.start()
    for copy in first:
        copy.wait()
    summed = source[mine, :].astype(F32)
    for k in range(3):
        summed = summed + slots[k].astype(F32)
    result[mine, :] = summed.astype(BF)
    for copy in second:
        copy.start()
    for copy in second:
        copy.wait()


def grid_sum(partial_value, collective_id):
    rows, columns = partial_value.shape
    in_vmem = pl.BlockSpec(memory_space=pltpu.VMEM)
    return pl.pallas_call(
        grid_sum_kernel,
        out_shape=jax.ShapeDtypeStruct((rows, columns), BF),
        in_specs=[in_vmem],
        out_specs=in_vmem,
        scratch_shapes=[pltpu.VMEM((3, rows // 4, columns), BF)]
        + [pltpu.SemaphoreType.DMA((3,))] * 4,
        compiler_params=pltpu.CompilerParams(
            collective_id=collective_id,
            has_side_effects=True,
            vmem_limit_bytes=24 * 1024 * 1024,
        ),
        cost_estimate=pl.CostEstimate(
            flops=4 * rows * columns, bytes_accessed=24 << 20, transcendentals=0
        ),
    )(partial_value)


def group_sum_kernel(count, source, small, result, small_out, slots, small_slots, total, *sems):
    group = lax.axis_index("dp")
    place = lax.axis_index("row") * 2 + lax.axis_index("col")

    def peers(k):
        return {"dp": lax.rem(group + k, count)}

    greet([peers(k) for k in range(1, count)] + [grid_device(k) for k in range(1, 4)])
    first, second, mine = exchange(source, slots, result, sems[:4], peers, group, count, "dp")
    send_small, recv_small, send_grid, recv_grid = sems[4:]
    small_first = [
        pltpu.make_async_remote_copy(
            src_ref=small,
            dst_ref=small_slots.at[k - 1],
            send_sem=send_small.at[k - 1],
            recv_sem=recv_small.at[k - 1],
            device_id=peers(k),
            device_id_type=pl.DeviceIdType.MESH,
        )
        for k in range(1, count)
    ]
    small_second = [
        pltpu.make_async_remote_copy(
            src_ref=total,
            dst_ref=small_out.at[place],
            send_sem=send_grid.at[k - 1],
            recv_sem=recv_grid.at[k - 1],
            device_id=grid_device(k),
            device_id_type=pl.DeviceIdType.MESH,
        )
        for k in range(1, 4)
    ]
    for copy in small_first + first:
        copy.start()
    for copy in small_first:
        copy.wait()
    gathered = jnp.zeros(small.shape, F32)
    for at in range(count):
        back = lax.rem(group - at + count, count)
        other = small_slots[jnp.maximum(back - 1, 0)]
        gathered = gathered + jnp.where(back == 0, small[...], other)
    total[...] = gathered
    small_out[place] = gathered
    for copy in small_second:
        copy.start()
    for copy in first:
        copy.wait()
    summed = source[mine, :].astype(F32)
    for k in range(count - 1):
        summed = summed + slots[k].astype(F32)
    result[mine, :] = summed.astype(BF)
    for copy in second:
        copy.start()
    for copy in small_second + second:
        copy.wait()


def group_sum(grads, small, groups):
    rows, columns = grads.shape
    if groups > 8 or rows % (16 * groups):
        return lax.psum(grads, "dp"), lax.all_gather(lax.psum(small, "dp"), GRID)
    in_vmem = pl.BlockSpec(memory_space=pltpu.VMEM)
    return pl.pallas_call(
        functools.partial(group_sum_kernel, groups),
        out_shape=(
            jax.ShapeDtypeStruct(grads.shape, BF),
            jax.ShapeDtypeStruct((4,) + small.shape, F32),
        ),
        in_specs=[in_vmem] * 2,
        out_specs=(in_vmem, in_vmem),
        scratch_shapes=[
            pltpu.VMEM((groups - 1, rows // groups, columns), BF),
            pltpu.VMEM((groups - 1,) + small.shape, F32),
            pltpu.VMEM(small.shape, F32),
        ]
        + [pltpu.SemaphoreType.DMA((groups - 1,))] * 6
        + [pltpu.SemaphoreType.DMA((3,))] * 2,
        compiler_params=pltpu.CompilerParams(
            collective_id=3, has_side_effects=True, vmem_limit_bytes=24 * 1024 * 1024
        ),
        cost_estimate=pl.CostEstimate(
            flops=8 * rows * columns, bytes_accessed=100 << 20, transcendentals=0
        ),
    )(grads, small)


def from_behind(array, by, groups):
    return lax.ppermute(
        array, "dp", [(i, i + by) for i in range(groups) if 0 <= i + by < groups]
    )


def shards(
    block_in,
    lengths,
    attend_in,
    query_bias,
    value_bias,
    attend_out,
    out_bias,
    gain_first,
    shift_first,
    gain_second,
    shift_second,
    up_weight,
    up_bias,
    down_weight,
    down_bias,
    grad_out,
):
    row = lax.axis_index("row")
    col = lax.axis_index("col")
    place = row * 2 + col
    group = lax.axis_index("dp")
    groups = lax.axis_size("dp")
    tokens, model = block_in.shape
    size = model // H
    heads = H // 4
    share = model // 4
    half = model // 2
    longest = min(LONGEST, tokens * groups // 2)
    visits = min((longest - 2 + tokens) // tokens, groups - 1)
    window = (visits + 1) * tokens
    top = row == 0
    left = col == 0

    crossing = lax.ppermute(attend_in[:, half : 2 * half], "row", SWAP)
    low, high = attend_in[:, :half], attend_in[:, 2 * half :]
    q_half = jnp.where(top, low, crossing)
    k_half = jnp.where(top, high, low)
    v_half = jnp.where(top, crossing, high)
    in_mine = jnp.concatenate([cut(w, col, share, 1) for w in (q_half, k_half, v_half)], axis=1)
    in_other = jnp.concatenate(
        [cut(w, 1 - col, share, 1) for w in (q_half, k_half, v_half)], axis=1
    )
    in_other = lax.ppermute(in_other, "col", SWAP)
    in_own = jnp.concatenate(
        [jnp.where(left, in_mine, in_other), jnp.where(left, in_other, in_mine)], axis=0
    )

    hidden_share = up_weight.shape[1] // 2
    up_mine = cut(up_weight, col, hidden_share, 1)
    up_other = lax.ppermute(cut(up_weight, 1 - col, hidden_share, 1), "col", SWAP)
    up_own = jnp.concatenate(
        [jnp.where(left, up_mine, up_other), jnp.where(left, up_other, up_mine)], axis=0
    )

    def rows_of(at):
        return jnp.concatenate(
            [cut(attend_out, at, share, 0), cut(down_weight, at, hidden_share, 0)], axis=0
        )

    part_a = lax.ppermute(rows_of(row), GRID, TRANSPOSE)
    part_b = lax.ppermute(rows_of(1 - row), GRID, TO_FLIPPED)
    rows_own = jnp.concatenate(
        [jnp.where(left, part_a, part_b), jnp.where(left, part_b, part_a)], axis=1
    )
    out_own, down_own = rows_own[:share], rows_own[share:]

    bounds = jnp.cumsum(lengths)
    everywhere = jnp.arange(tokens * groups, dtype=jnp.int32)
    starts = jnp.max(
        jnp.where(bounds[None, :] <= everywhere[:, None], bounds[None, :], 0), axis=1
    )
    start_own = cut(starts, group, tokens, 0)

    stream = block_in.astype(F32)
    n_first, inverse_first = normalise(stream)
    h_first = (n_first * gain_first + shift_first).astype(BF)
    bias_own = jnp.concatenate(
        [
            cut(query_bias, place, share, 0),
            jnp.zeros((share,), F32),
            cut(value_bias, place, share, 0),
        ]
    )
    qkv = (mm(h_first, in_own) + bias_own).astype(BF)
    queries, pair = qkv[:, :share], qkv[:, share:]
    pair, grad_out = lax.optimization_barrier((pair, grad_out))
    grad_full = lax.all_gather(grad_out, GRID, axis=1, tiled=True)
    pairs = jnp.concatenate(
        [from_behind(pair, by, groups) for by in range(visits, 0, -1)] + [pair], axis=0
    )
    key_base = jnp.stack([(group - visits) * tokens, group * tokens])
    shape = dict(heads=heads, size=size, rows=128)
    work = 4 * tokens * window * share
    mixed, log_total = local_kernel(
        functools.partial(forward_kernel, **shape),
        (
            jax.ShapeDtypeStruct((tokens, share), BF),
            jax.ShapeDtypeStruct((tokens, heads), F32),
        ),
        (key_base, queries, pairs, start_own[:, None]),
        work,
    )
    branch = grid_sum(mm(mixed, out_own).astype(BF), 1).astype(F32) + out_bias
    r_first = stream + branch

    n_second, inverse_second = normalise(r_first)
    h_second = (n_second * gain_second + shift_second).astype(BF)
    gate_in = mm(h_second, up_own) + cut(up_bias, place, hidden_share, 0)
    hidden32, gate_pull = jax.vjp(smooth_gate, gate_in)
    hidden = hidden32.astype(BF)
    down_share = lax.psum_scatter(
        mm(hidden, down_own).astype(BF), GRID, scatter_dimension=1, tiled=True
    ).astype(F32)
    block_out = cut(r_first, place, share, 1) + (down_share + cut(down_bias, place, share, 0))

    d_gate = gate_pull(mm_nt(grad_full, down_own))[0].astype(BF)
    d_second = grid_sum(mm_nt(d_gate, up_own).astype(BF), 2).astype(F32)

    own_qo = jnp.concatenate([queries, mixed], axis=1)
    later_qo = jnp.concatenate(
        [own_qo] + [from_behind(own_qo, -by, groups) for by in range(1, visits + 1)], axis=0
    )
    own_log = log_total.T
    later_log = jnp.concatenate(
        [own_log] + [from_behind(own_log, -by, groups) for by in range(1, visits + 1)], axis=1
    )
    beyond = jnp.full((tokens * visits,), tokens * groups, jnp.int32)
    later_start = lax.dynamic_slice_in_dim(
        jnp.concatenate([starts, beyond]), group * tokens, window, 0
    )[None, :]

    acts = jnp.concatenate([hidden, mixed], axis=1)
    acts_a = lax.ppermute(acts, GRID, TRANSPOSE)
    acts_b = lax.ppermute(acts, GRID, FROM_FLIPPED)
    d_second, later_qo, later_log, acts_a, acts_b = lax.optimization_barrier(
        (d_second, later_qo, later_log, acts_a, acts_b)
    )
    acts_0 = jnp.where(top, acts_a, acts_b)
    acts_1 = jnp.where(top, acts_b, acts_a)
    hidden_half = jnp.concatenate([acts_0[:, :hidden_share], acts_1[:, :hidden_share]], axis=1)
    mixed_half = jnp.concatenate([acts_0[:, hidden_share:], acts_1[:, hidden_share:]], axis=1)
    d_gate_half = lax.all_gather(d_gate, "col", axis=1, tiled=True)

    g_down = mm_tn(hidden_half, cut(grad_full, row, half, 1)).astype(BF)
    g_up = mm_tn(cut(h_second, col, half, 1), d_gate_half).astype(BF)
    d_second, g_down, g_up = lax.optimization_barrier((d_second, g_down, g_up))
    g_down, g_up = lax.psum((g_down, g_up), "dp")

    e_second = d_second * gain_second
    d_norm = inverse_second * (
        e_second
        - jnp.mean(e_second, axis=1, keepdims=True)
        - n_second * jnp.mean(e_second * n_second, axis=1, keepdims=True)
    )
    d_r_first = grad_full.astype(F32) + d_norm
    d_branch = d_r_first.astype(BF)
    d_mixed = mm_nt(d_branch, out_own).astype(BF)

    later_d = jnp.concatenate(
        [d_mixed] + [from_behind(d_mixed, -by, groups) for by in range(1, visits + 1)], axis=0
    )
    delta = jnp.sum(
        (d_mixed.astype(F32) * mixed.astype(F32)).reshape(tokens, heads, size), axis=2
    )
    d_query = local_kernel(
        functools.partial(query_kernel, **shape),
        jax.ShapeDtypeStruct((tokens, share), BF),
        (key_base, queries, pairs, start_own[:, None], log_total, delta, d_mixed),
        6 * tokens * window * share,
    )
    later_delta = jnp.sum(
        (later_d.astype(F32) * later_qo[:, share:].astype(F32)).reshape(window, heads, size),
        axis=2,
    ).T
    d_pair = local_kernel(
        functools.partial(key_kernel, **shape),
        jax.ShapeDtypeStruct((tokens, 2 * share), BF),
        (
            jnp.stack([group * tokens, group * tokens]),
            later_qo,
            later_d,
            pair,
            later_start,
            later_log,
            later_delta,
        ),
        8 * tokens * window * share,
    )
    d_pair, d_query, g_down, g_up = lax.optimization_barrier((d_pair, d_query, g_down, g_up))
    d_keys, d_values = d_pair[:, :share], d_pair[:, share:]
    d_qkv = jnp.concatenate([d_query, d_pair], axis=1)

    d_first = mm_nt(d_qkv, in_own)
    e_part = d_first * gain_first
    stats = jnp.concatenate(
        [
            jnp.sum(e_part, axis=1, keepdims=True),
            jnp.sum(e_part * n_first, axis=1, keepdims=True),
            jnp.zeros((tokens, 62), F32),
        ],
        axis=1,
    )
    sent = jnp.concatenate(
        [
            piece
            for at in range(4)
            for piece in (d_first[:, at * share : (at + 1) * share], stats)
        ],
        axis=1,
    ).astype(BF)
    d_share = lax.psum_scatter(sent, GRID, scatter_dimension=1, tiled=True).astype(F32)
    mean_e = d_share[:, share : share + 1] / model
    mean_en = d_share[:, share + 1 : share + 2] / model
    d_share = d_share[:, :share]
    n_share = cut(n_first, place, share, 1)
    grad_in = (
        cut(d_r_first, place, share, 1)
        + inverse_first * (d_share * cut(gain_first, place, share, 0) - mean_e - n_share * mean_en)
    ).astype(BF)

    moved = lax.ppermute(jnp.where(top, d_values, d_query), "row", SWAP)
    kept = jnp.concatenate(
        [jnp.where(top, d_query, d_keys), moved, jnp.where(top, d_keys, d_values)], axis=1
    )
    both = lax.all_gather(kept, "col", axis=0, tiled=False)
    d_cols = both.reshape(2, tokens, 3, share).transpose(1, 2, 0, 3).reshape(tokens, 3 * half)
    g_in = mm_tn(cut(h_first, col, half, 1), d_cols).astype(BF)
    g_out = mm_tn(mixed_half, cut(d_branch, row, half, 1)).astype(BF)

    def total(array):
        return jnp.sum(array, axis=0, dtype=F32)

    def own(vector):
        return cut(vector, place, vector.shape[0] // 4, 0)

    quarters = [
        total(d_query),
        total(d_values),
        own(total(d_branch)),
        own(total(d_second * n_second)),
        own(total(d_second)),
        own(total(grad_full)),
        total(d_gate),
    ]
    sums = [total(d_first * n_first), total(d_first)]
    lanes = 128
    quarter_size = 6 * share + hidden_share
    padding = jnp.zeros((40 * lanes - quarter_size - 2 * model,), F32)
    small = jnp.concatenate(quarters + sums + [padding]).reshape(40, lanes)
    grads, small = group_sum(jnp.concatenate([g_in, g_out], axis=1), small, groups)
    g_in, g_out = grads[:, : 3 * half], grads[:, 3 * half :]
    small = small.reshape(4, 40 * lanes)
    wholes = [small[:, at * share : (at + 1) * share].reshape(model) for at in range(6)]
    g_up_bias = small[:, 6 * share : quarter_size].reshape(4 * hidden_share)
    g_down_bias = wholes[5]
    firsts = jnp.sum(small[:, quarter_size : quarter_size + 2 * model], axis=0)
    parts = wholes[:3] + [firsts[:model], firsts[model:]] + wholes[3:5]
    return (
        block_out,
        grad_in,
        g_in.astype(F32),
        parts[0],
        parts[1],
        g_out.astype(F32),
        parts[2],
        parts[3],
        parts[4],
        parts[5],
        parts[6],
        g_up.astype(F32),
        g_up_bias,
        g_down.astype(F32),
        g_down_bias,
    )


def solution(mesh):
    placed = (
        P("dp", None),
        P(),
        P("col", "row"),
        P(),
        P(),
        P("col", "row"),
        P(),
        P(),
        P(),
        P(),
        P(),
        P("col", "row"),
        P(),
        P("col", "row"),
        P(),
        P("dp", ("row", "col")),
    )
    return jax.shard_map(
        shards,
        mesh=mesh,
        in_specs=placed,
        out_specs=(
            P("dp", ("row", "col")),
            P("dp", ("row", "col")),
            P("col", "row"),
            P(),
            P(),
            P("col", "row"),
            P(),
            P(),
            P(),
            P(),
            P(),
            P("col", "row"),
            P(),
            P("col", "row"),
            P(),
        ),
        check_vma=False,
    )
```
